256 devices in a mesh: blk: 32 (over y_lo, z, core), dp: 8 (over x, y_hi).
Axes of the slice: x: 4, y: 4 (y_hi: 2, y_lo: 2; y = y_hi * 2 + y_lo), z: 8, core: 2. Of those that a mesh axis runs over, the one named last changes fastest.
Arguments:
- residuals: bfloat16 [32768, 768], P(('blk', 'dp')), may hold values from -130 to 130
- codebook: bfloat16 [24576, 768], P('blk'), may hold values from -9 to 9
- section_codes: int32 [32768], P(('blk', 'dp')), may hold values from 0 to 1023, as said below
- code_owner: int32 [1024], replicated, may hold values from 0 to 31, as said below
Outputs:
- new_codebook: float32 [24576, 768], P('blk')
- code_shift: float32 [2048, 768], P('blk')
The draws below stay inside these ranges and needn't reach their ends.
Inputs may be any that keep to these rules, and one draw needn't show every extreme that they name: `section_codes`: among the rows of one device, at most 12 have section-one codes owned by one codeword block, and in every device's rows some block is named exactly 12 times. `code_owner`: each codeword block owns at least one and at most 64 section-one codes; some block owns exactly 64.
All inputs are finite; a program needn't handle non-finite values.
Results may differ from the reference program's by a relative error of at most 0.002.
Values may be sent and summed in bfloat16 or wider, within the bound.
No kernel may reach another device: no remote copies, remote signals or barrier semaphores. Data moves between devices by JAX's collectives and lax.ppermute only.
A program may use at most 128 MiB of HBM per device.

```python
import math
import jax
import jax.numpy as jnp
from jax import lax

D = 768
CB_DEV = 768
ROW_DEV = 128
K = 24576
ROWS = 32768
CODES = 1024
SLOTS = 64
CAP = 12
SHIFTS = 2048
N_BLK = 32


def codebook_values(key):
    base = jnp.clip(jax.random.normal(jax.random.fold_in(key, 101), (K, D), jnp.float32), -6.0, 6.0)
    base = base.astype(jnp.bfloat16).astype(jnp.float32)
    index = jnp.arange(K, dtype=jnp.int32)
    previous = jnp.roll(base, 1, axis=0)
    paired = jnp.where((index % 64 == 1)[:, None], previous * 1.01, base)
    return paired.astype(jnp.bfloat16).astype(jnp.float32)


def layout(key):
    nblk = K // CB_DEV
    total_slots = nblk * SLOTS
    slot = jnp.arange(total_slots, dtype=jnp.int32)
    slot_owner = slot // SLOTS
    full_owner = jax.random.randint(jax.random.fold_in(key, 201), (), 0, nblk)
    forced = (slot_owner == full_owner) | (slot % SLOTS == 0)
    prior = jnp.where(forced, 0, 1 + jax.random.randint(jax.random.fold_in(key, 202), (total_slots,), 0, 1 << 14))
    order = jnp.argsort(prior * total_slots + slot)[:CODES]
    mixing = jax.random.permutation(jax.random.fold_in(key, 203), CODES)
    code_owner = slot_owner[order][mixing].astype(jnp.int32)
    by_owner = jnp.argsort(code_owner, stable=True).astype(jnp.int32)
    counts = jnp.sum((code_owner[None, :] == jnp.arange(nblk, dtype=jnp.int32)[:, None]).astype(jnp.int32), axis=1)
    starts = jnp.cumsum(counts) - counts
    pool = nblk * CAP
    blocks = ROWS // ROW_DEV

    def one_block(block_key):
        heavy = jax.random.randint(jax.random.fold_in(block_key, 1), (), 0, nblk)
        weight = 1 + jax.random.randint(jax.random.fold_in(block_key, 2), (nblk,), 0, 8)
        place = jnp.arange(pool, dtype=jnp.int32)
        place_owner = place // CAP
        scored = 1 + jax.random.randint(jax.random.fold_in(block_key, 3), (pool,), 0, 1 << 14) // weight[place_owner]
        scored = jnp.where(place_owner == heavy, 0, scored)
        chosen = jnp.argsort(scored * pool + place)[:ROW_DEV]
        owners = place_owner[chosen][jax.random.permutation(jax.random.fold_in(block_key, 4), ROW_DEV)]
        picked = starts[owners] + jax.random.randint(jax.random.fold_in(block_key, 5), (ROW_DEV,), 0, counts[owners])
        return by_owner[picked]
    block_keys = jax.vmap(lambda index: jax.random.fold_in(key, 300 + index))(jnp.arange(blocks, dtype=jnp.int32))
    codes = jax.vmap(one_block)(block_keys).reshape(-1).astype(jnp.int32)
    return (code_owner, codes)


def draw_codebook(key, part):
    return codebook_values(key).astype(jnp.bfloat16)


def draw_residuals(key, part):
    base = jnp.clip(jax.random.normal(jax.random.fold_in(key, 111), (ROWS, D), jnp.float32), -6.0, 6.0)
    table = codebook_values(key)
    index = jnp.arange(ROWS, dtype=jnp.int32)
    first = 64 * jax.random.randint(jax.random.fold_in(key, 115), (ROWS,), 0, K // 64)
    level = 110.0 + 60.0 * (index % 3).astype(jnp.float32)
    strength = 0.5 * (level / math.sqrt(D) + 1.0)
    aligned = strength[:, None] * table[first]
    base = jnp.where((index % 61 == 0)[:, None], aligned, base)
    return base.astype(jnp.bfloat16)


def draw_section_codes(key, part):
    return layout(key)[1]


def draw_code_owner(key, part):
    return layout(key)[0]


def setup_inputs(seed: int = 0) -> dict:
    arg_keys = jax.random.split(jax.random.key(seed), 5)
    return {
        "residuals": draw_residuals(jax.random.fold_in(arg_keys[4], 71), 0),
        "codebook": draw_codebook(jax.random.fold_in(arg_keys[4], 71), 0),
        "section_codes": draw_section_codes(jax.random.fold_in(arg_keys[4], 71), 0),
        "code_owner": draw_code_owner(jax.random.fold_in(arg_keys[4], 71), 0),
    }


def reference(residuals, codebook, section_codes, code_owner):
    factor = 2.0 / math.sqrt(D)
    cb_float = codebook.astype(jnp.float32)
    half_norm = 0.5 * lax.optimization_barrier(jnp.sum(cb_float * cb_float, axis=1))
    stacked = residuals.reshape(ROWS // ROW_DEV, ROW_DEV, D)

    def one_block(carry, rows):
        raw = jnp.dot(rows, codebook.T, preferred_element_type=jnp.float32)
        scores = (raw - half_norm[None, :]) * factor
        top = lax.optimization_barrier(jnp.max(scores, axis=1))
        expo = jnp.exp(scores - top[:, None])
        total = lax.optimization_barrier(jnp.sum(expo, axis=1))
        weights = (expo / total[:, None]).astype(jnp.bfloat16)
        weighted = carry[0] + jnp.dot(weights.T, rows, preferred_element_type=jnp.float32)
        mass = carry[1] + lax.optimization_barrier(jnp.sum(weights.astype(jnp.float32), axis=0))
        return ((weighted, mass), None)
    start = (jnp.zeros((K, D), jnp.float32), jnp.zeros((K,), jnp.float32))
    (weighted, mass), _ = lax.scan(one_block, start, stacked)
    new_codebook = (weighted + 0.5 * cb_float) / (mass + 0.5)[:, None]
    owner_hot = (code_owner[:, None] == jnp.arange(N_BLK, dtype=jnp.int32)[None, :]).astype(jnp.int32)
    before = jnp.cumsum(owner_hot, axis=0) - owner_hot
    rank = lax.optimization_barrier(jnp.sum(before * owner_hot, axis=1)).astype(jnp.int32)
    code_slot = (code_owner * SLOTS + rank).astype(jnp.int32)
    row_slot = jnp.take(code_slot, section_codes).astype(jnp.int32)
    shift_sum = jax.ops.segment_sum(residuals.astype(jnp.float32), row_slot, num_segments=SHIFTS)
    shift_count = jax.ops.segment_sum(jnp.ones((ROWS,), jnp.float32), row_slot, num_segments=SHIFTS)
    code_shift = shift_sum / (shift_count + 1.0)[:, None]
    return (new_codebook, code_shift)
```

```python
import functools
import math

import jax
import jax.numpy as jnp
from jax import lax
from jax.experimental import pallas as pl
from jax.experimental.pallas import tpu as pltpu
from jax.sharding import PartitionSpec as P

SLOTS = 64
X, Y, Z, C = 4, 4, 8, 2
PEERS = X * Y // 2
AXES = ("blk", "dp")
PRIOR = 0.5
MIB = 1 << 20


def place(x, y, z, c):
    return ((y % 2 * Z + z) * C + c) * PEERS + x * 2 + y // 2


def chips():
    for x in range(X):
        for y in range(Y):
            for z in range(Z):
                for c in range(C):
                    yield x, y, z, c


def shifted(value, dy=0, dz=0, dc=0):
    pairs = [
        (place(x, y, z, c), place(x, (y + dy) % Y, (z + dz) % Z, (c + dc) % C)) for x, y, z, c in chips()
    ]
    return lax.ppermute(value, AXES, pairs)


def z_partner(value, bit):
    pairs = [(place(x, y, z, c), place(x, y, z ^ bit, c)) for x, y, z, c in chips()]
    return lax.ppermute(value, AXES, pairs)


def score_kernel(count, *refs):
    codebook, half_norm = refs[:2]
    rows = refs[2 : 2 + count]
    expo, stats = refs[2 + count :]
    factor = 2.0 / math.sqrt(codebook.shape[1])
    at = 0
    for block in rows:
        n = block.shape[0]
        raw = lax.dot_general(
            codebook[...], block[...], (((1,), (1,)), ((), ())), preferred_element_type=jnp.float32
        )
        scores = (raw - half_norm[...]) * factor
        top = jnp.max(scores, axis=0, keepdims=True)
        value = jnp.exp(scores - top)
        expo[:, at : at + n] = value
        stats[0:1, at : at + n] = top
        stats[1:2, at : at + n] = jnp.sum(value, axis=0, keepdims=True)
        at += n


def score_rows(codebook, half_norm, rows):
    k, width = codebook.shape
    total = sum(r.shape[0] for r in rows)
    return pl.pallas_call(
        functools.partial(score_kernel, len(rows)),
        out_shape=(
            jax.ShapeDtypeStruct((k, total), jnp.float32),
            jax.ShapeDtypeStruct((2, total), jnp.float32),
        ),
        compiler_params=pltpu.CompilerParams(vmem_limit_bytes=24 * MIB),
        cost_estimate=pl.CostEstimate(
            flops=2 * k * width * total, bytes_accessed=2 * k * width + 4 * k * total, transcendentals=k * total
        ),
    )(codebook, half_norm, *rows)


def sum_kernel(layout, *refs):
    groups = len(layout)
    count = sum(len(g) for g in layout)
    expos = refs[:groups]
    rows = refs[groups : groups + count]
    scale, slots, weighted, mass, shift, hits = refs[groups + count :]
    k = weighted.shape[0]
    tile = 256

    def pieces():
        at, i = 0, 0
        for g, sizes in enumerate(layout):
            inner = 0
            for n in sizes:
                yield g, inner, at, n, rows[i]
                inner, at, i = inner + n, at + n, i + 1

    def folded(w):
        w = w.astype(jnp.float32)
        return sum(w[:, j : j + 128] for j in range(0, w.shape[1], 128))

    for t in range(0, k, tile):
        total = jnp.zeros((tile, weighted.shape[1]), jnp.float32)
        heavy = jnp.zeros((tile, 128), jnp.float32)
        for g, inner, at, n, block in pieces():
            w = (expos[g][t : t + tile, inner : inner + n] * scale[0:1, at : at + n]).astype(jnp.bfloat16)
            total += jnp.dot(w, block[...], preferred_element_type=jnp.float32)
            heavy += folded(w)
        weighted[t : t + tile, :] = total
        mass[t : t + tile, :] = jnp.sum(heavy, axis=1, keepdims=True)
    total = jnp.zeros(shift.shape, jnp.float32)
    heavy = jnp.zeros((SLOTS, 128), jnp.float32)
    for g, inner, at, n, block in pieces():
        want = lax.broadcasted_iota(jnp.int32, (SLOTS, n), 0)
        hot = jnp.where(want == slots[0:1, at : at + n], 1.0, 0.0).astype(jnp.bfloat16)
        total += jnp.dot(hot, block[...], preferred_element_type=jnp.float32)
        heavy += folded(hot)
    shift[...] = total
    hits[...] = jnp.sum(heavy, axis=1, keepdims=True)


def sum_rows(expos, rows, scale, slots):
    k = expos[0].shape[0]
    flat = [r for group in rows for r in group]
    width = flat[0].shape[1]
    total = sum(r.shape[0] for r in flat)
    return pl.pallas_call(
        functools.partial(sum_kernel, [[r.shape[0] for r in group] for group in rows]),
        out_shape=(
            jax.ShapeDtypeStruct((k, width), jnp.float32),
            jax.ShapeDtypeStruct((k, 1), jnp.float32),
            jax.ShapeDtypeStruct((SLOTS, width), jnp.float32),
            jax.ShapeDtypeStruct((SLOTS, 1), jnp.float32),
        ),
        compiler_params=pltpu.CompilerParams(vmem_limit_bytes=24 * MIB),
        cost_estimate=pl.CostEstimate(
            flops=2 * (k + SLOTS) * width * total, bytes_accessed=4 * k * total + 2 * width * total, transcendentals=0
        ),
    )(*expos, *flat, scale, slots)


def combine(first, second):
    top = jnp.maximum(first[0], second[0])
    total = first[1] * jnp.exp(first[0] - top) + second[1] * jnp.exp(second[0] - top)
    return jnp.stack([top, total, first[2] + second[2]])


def row_slots(section_codes, code_owner):
    codes = code_owner.shape[0]
    index = jnp.arange(codes, dtype=jnp.int32)
    same = (code_owner[:, None] == code_owner[None, :]) & (index[None, :] < index[:, None])
    code_slot = code_owner * SLOTS + jnp.sum(same.astype(jnp.int32), axis=1)
    hit = section_codes[:, None] == index[None, :]
    return jnp.sum(jnp.where(hit, code_slot[None, :], 0), axis=1)


def halved(rows):
    size = jnp.max(jnp.abs(rows), axis=-1, keepdims=True)
    exponent = jnp.clip(jnp.ceil(jnp.log2(jnp.maximum(size, 1e-30))), -100.0, 100.0)
    return (rows * jnp.exp2(-exponent)).astype(jnp.float16), exponent


def as_row(values, width):
    pad = [(0, 0)] * (values.ndim - 1) + [(0, width - values.shape[-1])]
    return jnp.pad(values, pad)[..., None, :].astype(jnp.float16)


def local(residuals, codebook, section_codes, code_owner):
    blk = lax.axis_index("blk")
    peer = lax.axis_index("dp")
    z, core = blk // C % Z, blk % C
    count, width = residuals.shape
    k = codebook.shape[0]
    half = count // 2

    start = jnp.concatenate(
        [residuals, shifted(residuals[:half], dy=1), shifted(residuals[half:], dy=-1)]
    )
    side = start.shape[0]
    up, down = [start], [start]
    for _ in range(Z // 2 - 1):
        up.append(shifted(up[-1], dz=1))
        down.append(shifted(down[-1], dz=-1))
    up.append(shifted(up[-1][: side // 2], dz=1))
    down.append(shifted(down[-1][side // 2 :], dz=-1))
    rounds = [[start]] + [[up[i], down[i]] for i in range(1, Z // 2 + 1)]
    rows = [[r for own in group for r in (own, shifted(own, dc=1))] for group in rounds]

    half_norm = 0.5 * jnp.sum(jnp.square(codebook.astype(jnp.float32)), axis=1, keepdims=True)
    scored = [score_rows(codebook, half_norm, group) for group in rows]
    expos = [s[0] for s in scored]

    by_z = [None] * Z
    by_z[0] = scored[0][1].reshape(2, 1, C, side)
    for i in range(1, Z // 2):
        pair = scored[i][1].reshape(2, 2, C, side)
        by_z[Z - i], by_z[i] = pair[:, :1], pair[:, 1:]
    last = scored[Z // 2][1].reshape(2, 2, C, side // 2)
    by_z[Z // 2] = jnp.concatenate([last[:, 0], last[:, 1]], axis=2)[:, None]
    near = jnp.concatenate(by_z, axis=1)

    def to_absolute(a):
        a = lax.dynamic_slice_in_dim(jnp.concatenate([a, a], axis=1), (Z - z) % Z, Z, axis=1)
        return jnp.where(core == 0, a, a[:, :, ::-1])

    def to_near(a):
        a = lax.dynamic_slice_in_dim(jnp.concatenate([a, a], axis=1), z, Z, axis=1)
        return jnp.where(core == 0, a, a[:, :, ::-1])

    slots = row_slots(section_codes, code_owner).astype(jnp.float32)
    own = (jnp.arange(Z)[:, None, None] == z) & (jnp.arange(C)[None, :, None] == core)
    mine = jnp.where(own, jnp.pad(slots, (0, side - count))[None, None, :], 0.0)
    stats = jnp.concatenate([to_absolute(near), mine[None]])

    a, b, c, d = (stats[..., i * half : (i + 1) * half] for i in range(4))
    from_up = shifted(jnp.concatenate([b, c], axis=-1), dy=-1)
    from_down = shifted(jnp.concatenate([a, d], axis=-1), dy=1)
    stats = combine(
        stats,
        jnp.concatenate(
            [from_up[..., half:], from_down[..., half:], from_down[..., :half], from_up[..., :half]], axis=-1
        ),
    )
    stats = combine(stats, shifted(stats, dc=1))
    for bit in (1, 2, 4):
        stats = combine(stats, z_partner(stats, bit))

    stats = to_near(stats)
    scale = jnp.exp(near[0] - stats[0]) / stats[1]
    slot_of = stats[2].astype(jnp.int32) - blk * SLOTS

    def in_order(a):
        out = [a[0].reshape(-1)]
        for i in range(1, Z // 2):
            out += [a[Z - i].reshape(-1), a[i].reshape(-1)]
        far = a[Z // 2]
        return jnp.concatenate(out + [far[:, : side // 2].reshape(-1), far[:, side // 2 :].reshape(-1)])[None]

    weighted, mass, shift, hits = sum_rows(expos, rows, in_order(scale), in_order(slot_of))

    part, slot_part = k // PEERS, SLOTS // PEERS
    sums = jnp.concatenate(
        [weighted.reshape(PEERS, part, width), shift.reshape(PEERS, slot_part, width)], axis=1
    )
    counts = jnp.concatenate([mass.reshape(PEERS, part), hits.reshape(PEERS, slot_part)], axis=1)
    packed, exponent = halved(sums)
    high = lax.reduce_precision(counts, 5, 10)
    lines = [as_row(v, width) for v in (exponent[..., 0], high, counts - high)]
    got = lax.all_to_all(
        jnp.concatenate([packed, *lines], axis=1), "dp", split_axis=0, concat_axis=0, tiled=True
    ).astype(jnp.float32)
    both = part + slot_part
    sums = jnp.sum(got[:, :both] * jnp.exp2(got[:, both, :both])[..., None], axis=0)
    counts = jnp.sum(got[:, both + 1, :both] + got[:, both + 2, :both], axis=0)[:, None]
    prior = PRIOR * lax.dynamic_slice_in_dim(codebook, peer * part, part).astype(jnp.float32)
    result = jnp.concatenate(
        [
            (sums[:part] + prior) / (counts[:part] + PRIOR),
            sums[part:] / (counts[part:] + 1.0),
        ]
    )
    packed, exponent = halved(result)
    sent = jnp.concatenate([packed, as_row(exponent[:, 0], width)])
    got = lax.all_to_all(
        jnp.broadcast_to(sent[None], (PEERS, *sent.shape)), "dp", split_axis=0, concat_axis=0, tiled=True
    ).astype(jnp.float32)
    result = got[:, :both] * jnp.exp2(got[:, both, :both])[..., None]
    return result[:, :part].reshape(k, width), result[:, part:].reshape(SLOTS, width)


def solution(mesh):
    in_specs = (P(("blk", "dp"), None), P("blk", None), P(("blk", "dp")), P())
    out_specs = (P("blk", None), P("blk", None))
    return jax.shard_map(local, mesh=mesh, in_specs=in_specs, out_specs=out_specs, check_vma=False)
```

```python
import functools
import math

import jax
import jax.numpy as jnp
from jax import lax
from jax.experimental import pallas as pl
from jax.experimental.pallas import tpu as pltpu
from jax.sharding import PartitionSpec as P

SLOTS = 64
X, Y, Z, C = 4, 4, 8, 2
PEERS = X * Y // 2
AXES = ("blk", "dp")
PRIOR = 0.5
MIB = 1 << 20
LANES = 128
TILE = 256


def place(x, y, z, c):
    return ((y % 2 * Z + z) * C + c) * PEERS + x * 2 + y // 2


def chips():
    for x in range(X):
        for y in range(Y):
            for z in range(Z):
                for c in range(C):
                    yield x, y, z, c


def shifted(value, dy=0, dz=0, dc=0):
    pairs = [
        (place(x, y, z, c), place(x, (y + dy) % Y, (z + dz) % Z, (c + dc) % C)) for x, y, z, c in chips()
    ]
    return lax.ppermute(value, AXES, pairs)


def lower_half():
    return lax.broadcasted_iota(jnp.int32, (Z, LANES), 1) < LANES // 2


def score_kernel(plan, count, *refs):
    books, norms, sources = refs[:2], refs[2:4], refs[4 : 4 + count]
    expos, rows, stats = refs[4 + count : 6 + count], refs[6 + count], refs[7 + count]
    k, width = books[0].shape
    n = rows.shape[0]
    for s, a, m, b in plan:
        rows[b : b + m, :] = sources[s][a : a + m, :]
    factor = 2.0 / math.sqrt(width)
    for at in range(0, n, TILE):
        m = min(TILE, n - at)
        block = rows[at : at + m, :]
        scores = [
            (
                lax.dot_general(
                    book[...], block, (((1,), (1,)), ((), ())), preferred_element_type=jnp.float32
                )
                - norm[...]
            )
            * factor
            for book, norm in zip(books, norms)
        ]
        top = jnp.maximum(*(jnp.max(part, axis=0, keepdims=True) for part in scores))
        total = jnp.zeros((1, m), jnp.float32)
        for part, expo in zip(scores, expos):
            value = jnp.exp(part - top)
            total += jnp.sum(value, axis=0, keepdims=True)
            expo[:, at : at + m] = value.astype(jnp.bfloat16)
        for j in range(0, m, LANES):
            g = (at + j) // LANES
            stats[0, g : g + 1, :] = top[:, j : j + LANES]
            stats[1, g : g + 1, :] = total[:, j : j + LANES]


def score_rows(books, norms, sources, plan):
    k, width = books[0].shape
    n = sum(p[2] for p in plan)
    whole = pl.BlockSpec(memory_space=pltpu.VMEM)
    return pl.pallas_call(
        functools.partial(score_kernel, plan, len(sources)),
        in_specs=[whole] * (4 + len(sources)),
        out_specs=(whole,) * 4,
        out_shape=(
            jax.ShapeDtypeStruct((k, n), jnp.bfloat16),
            jax.ShapeDtypeStruct((k, n), jnp.bfloat16),
            jax.ShapeDtypeStruct((n, width), jnp.bfloat16),
            jax.ShapeDtypeStruct((2, n // LANES, LANES), jnp.float32),
        ),
        compiler_params=pltpu.CompilerParams(vmem_limit_bytes=20 * MIB),
        cost_estimate=pl.CostEstimate(
            flops=4 * k * width * n, bytes_accessed=4 * k * width + 4 * k * n, transcendentals=2 * k * n
        ),
    )(*books, *norms, *sources)


def arrange_kernel(groups, position, slots, *refs):
    stats, (out, near, far) = refs[:-3], refs[-3:]
    z = position[0]
    out[2] = jnp.zeros((2, Z, LANES), jnp.float32)
    for which in range(2):
        g = 0
        for stage in stats:
            for i in range(stage.shape[1]):
                side, off = groups[g]
                at = lax.rem(z + off, Z)
                (near, far)[side][pl.ds(at, 1), :] = stage[which, i : i + 1, :]
                g += 1
        out[which, 0] = jnp.where(lower_half(), near[...], far[...])
        out[which, 1] = jnp.where(lower_half(), far[...], near[...])
    first = lax.broadcasted_iota(jnp.int32, (1, LANES), 1) < LANES // 2
    out[2, 0, pl.ds(z, 1), :] = jnp.where(first, slots[...], 0.0)
    out[2, 1, pl.ds(z, 1), :] = jnp.where(first, 0.0, slots[...])


def arrange(groups, position, slots, stats):
    return pl.pallas_call(
        functools.partial(arrange_kernel, groups),
        in_specs=[pl.BlockSpec(memory_space=pltpu.SMEM)]
        + [pl.BlockSpec(memory_space=pltpu.VMEM)] * (1 + len(stats)),
        out_specs=pl.BlockSpec(memory_space=pltpu.VMEM),
        out_shape=jax.ShapeDtypeStruct((3, 2, Z, LANES), jnp.float32),
        scratch_shapes=[pltpu.VMEM((Z, LANES), jnp.float32)] * 2,
        compiler_params=pltpu.CompilerParams(vmem_limit_bytes=4 * MIB),
    )(position, slots, *stats)


def sum_kernel(groups, sizes, position, near, parts, *refs):
    stages = len(sizes)
    expo_in, rows_in = refs[:stages], refs[stages : 2 * stages]
    sums, counts = refs[2 * stages : 2 * stages + 2]
    weights, rows, scale, slot = refs[2 * stages + 2 :]
    k, width = expo_in[0].shape[0], rows.shape[1]
    n = rows.shape[0]
    part, each = k // PEERS, SLOTS // PEERS
    z, first_slot = position[0], position[1]

    def unfolded(pair):
        return jnp.where(lower_half(), pair[0], pair[1]), jnp.where(lower_half(), pair[1], pair[0])

    ratio, number = [], []
    for i in range(2):
        top = functools.reduce(jnp.maximum, [parts[j, 0, i] for j in range(Z)])
        whole = sum(parts[j, 1, i] * jnp.exp(parts[j, 0, i] - top) for j in range(Z))
        ratio.append(jnp.exp(near[0, i] - top) / whole)
        number.append(sum(parts[j, 2, i] for j in range(Z)))
    scale[0], scale[1] = unfolded(ratio)
    slot[0], slot[1] = unfolded(number)

    def line(ref, g):
        side, off = groups[g]
        return ref[side, pl.ds(lax.rem(z + off, Z), 1), :]

    heavy = jnp.zeros((k, LANES), jnp.float32)
    hits = jnp.zeros((LANES, LANES), jnp.float32)
    want = lax.broadcasted_iota(jnp.int32, (LANES, LANES), 0) + first_slot
    total = None
    at, g, done = 0, 0, 0
    for s in range(stages):
        rows[at : at + sizes[s], :] = rows_in[s][...]
        for j in range(0, sizes[s], LANES):
            w = (expo_in[s][:, j : j + LANES].astype(jnp.float32) * line(scale, g)).astype(jnp.bfloat16)
            heavy += w.astype(jnp.float32)
            weights[:k, at + j : at + j + LANES] = w
            hot = jnp.where(want == line(slot, g).astype(jnp.int32), 1.0, 0.0)
            hits += hot
            weights[k:, at + j : at + j + LANES] = hot[:SLOTS].astype(jnp.bfloat16)
            g += 1
        at += sizes[s]
        upto = n if s == stages - 1 else at // TILE * TILE
        if upto - done >= 2 * TILE or upto == n:
            add = jnp.dot(weights[:, done:upto], rows[done:upto, :], preferred_element_type=jnp.float32)
            total = add if total is None else total + add
            done = upto
    for p in range(PEERS):
        sums[p, :part, :] = total[p * part : (p + 1) * part, :]
        sums[p, part:, :] = total[k + p * each : k + (p + 1) * each, :]
    mass = jnp.sum(heavy.T, axis=0, keepdims=True)
    hits = jnp.sum(hits.T, axis=0, keepdims=True)
    blank = jnp.zeros((1, LANES - part - each), jnp.float32)
    for p in range(PEERS):
        counts[p : p + 1, :] = jnp.concatenate(
            [mass[:, p * part : (p + 1) * part], hits[:, p * each : (p + 1) * each], blank], axis=1
        )


def sum_rows(groups, position, near, parts, expos, rows):
    k = expos[0].shape[0]
    width = rows[0].shape[1]
    sizes = tuple(r.shape[0] for r in rows)
    n = sum(sizes)
    in_vmem = pl.BlockSpec(memory_space=pltpu.VMEM)
    return pl.pallas_call(
        functools.partial(sum_kernel, groups, sizes),
        in_specs=[pl.BlockSpec(memory_space=pltpu.SMEM)] + [in_vmem] * (2 + 2 * len(sizes)),
        out_specs=(in_vmem, in_vmem),
        out_shape=(
            jax.ShapeDtypeStruct((PEERS, (k + SLOTS) // PEERS, width), jnp.float32),
            jax.ShapeDtypeStruct((PEERS, LANES), jnp.float32),
        ),
        scratch_shapes=[
            pltpu.VMEM((k + SLOTS, n), jnp.bfloat16),
            pltpu.VMEM((n, width), jnp.bfloat16),
            pltpu.VMEM((2, Z, LANES), jnp.float32),
            pltpu.VMEM((2, Z, LANES), jnp.float32),
        ],
        compiler_params=pltpu.CompilerParams(vmem_limit_bytes=20 * MIB),
        cost_estimate=pl.CostEstimate(
            flops=2 * (k + SLOTS) * width * n, bytes_accessed=2 * k * n + 2 * width * n, transcendentals=0
        ),
    )(position, near, parts, *expos, *rows)


def pack_kernel(kept, taken, kept_counts, taken_counts, out):
    count, width = kept.shape[1:]
    at = count * (width // LANES)
    counts = kept_counts[...] + taken_counts[...]
    high = counts.astype(jnp.bfloat16).astype(jnp.float32)
    low = counts - high
    for p in range(PEERS):
        rows = kept[p] + taken[p]
        size = jnp.max(jnp.abs(rows), axis=1, keepdims=True)
        exponent = jnp.clip(jnp.ceil(jnp.log2(jnp.maximum(size, 1e-30))), -100.0, 100.0)
        rows = rows * jnp.exp2(-exponent)
        for b in range(width // LANES):
            out[p, b * count : (b + 1) * count, :] = rows[:, b * LANES : (b + 1) * LANES]
        wide = jnp.concatenate(
            [jnp.broadcast_to(exponent, (count, LANES)), jnp.zeros((LANES - count, LANES), jnp.float32)]
        )
        out[p, at : at + 1, :] = wide.T[:1, :]
        out[p, at + 1 : at + 2, :] = high[p : p + 1, :]
        out[p, at + 2 : at + 3, :] = low[p : p + 1, :]


def packed_sums(kept, taken):
    _, count, width = kept[0].shape
    in_vmem = pl.BlockSpec(memory_space=pltpu.VMEM)
    return pl.pallas_call(
        pack_kernel,
        in_specs=[in_vmem] * 4,
        out_specs=in_vmem,
        out_shape=jax.ShapeDtypeStruct((PEERS, count * (width // LANES) + 3, LANES), jnp.float32),
        compiler_params=pltpu.CompilerParams(vmem_limit_bytes=8 * MIB),
    )(kept[0], taken[0], kept[1], taken[1])


def combine(first, second):
    top = jnp.maximum(first[0], second[0])
    total = first[1] * jnp.exp(first[0] - top) + second[1] * jnp.exp(second[0] - top)
    return jnp.stack([top, total, first[2] + second[2]])


def row_slots(section_codes, code_owner):
    codes = code_owner.shape[0]
    index = jnp.arange(codes, dtype=jnp.int32)
    same = (code_owner[:, None] == code_owner[None, :]) & (index[None, :] < index[:, None])
    code_slot = code_owner * SLOTS + jnp.sum(same.astype(jnp.int32), axis=1)
    hit = section_codes[:, None] == index[None, :]
    return jnp.sum(jnp.where(hit, code_slot[None, :], 0), axis=1)


def as_row(values):
    pad = [(0, 0)] * (values.ndim - 1) + [(0, LANES - values.shape[-1])]
    return jnp.pad(values, pad)[..., None, :].astype(jnp.float16)


def local(residuals, codebook, section_codes, code_owner):
    blk = lax.axis_index("blk")
    peer = lax.axis_index("dp")
    z, core = blk // C % Z, blk % C
    count, width = residuals.shape
    k = codebook.shape[0]
    half = count // 2

    def norm(book):
        return 0.5 * jnp.sum(jnp.square(book.astype(jnp.float32)), axis=1, keepdims=True)

    up, down = shifted(residuals, dz=1), shifted(residuals, dz=-1)
    other = shifted(codebook, dc=1)
    books, norms = (codebook, other), (norm(codebook), norm(other))

    groups, scored = [], []

    def stage(same, sides):
        sources, plan, at = [], [], 0
        for block, off in same:
            for piece in block:
                plan.append((len(sources), 0, piece.shape[0], at))
                sources.append(piece)
                at += piece.shape[0]
            groups.append((0, off % Z))
        if sides:
            first = len(sources)
            sources.extend(sides[:2])
            for i, off in enumerate(sides[2]):
                plan += [(first, i * half, half, at), (first + 1, i * half, half, at + half)]
                at += count
                groups.append((1, off % Z))
        scored.append(score_rows(books, norms, sources, tuple(plan)))

    def after(value, *earlier):
        return lax.optimization_barrier((value, earlier))[0]

    def across(blocks, *earlier):
        parts = after(
            (jnp.concatenate([b[:half] for b in blocks]), jnp.concatenate([b[half:] for b in blocks])), *earlier
        )
        return shifted(parts[0], dy=1), shifted(parts[1], dy=-1)

    stage([([residuals], 0), ([up], -1), ([down], 1)], None)
    sides = [across([residuals, up, down], scored[-1][3])]
    up, down = shifted(up, dz=1), shifted(down, dz=-1)
    up, down = after((up, down), scored[-1][3])
    stage([([up], -2), ([down], 2)], None)
    sides.append(across([up, down], scored[-1][3]))
    up, down = shifted(up, dz=1), shifted(down, dz=-1)
    up, down = after((up, down), scored[-1][3], *sides[0])
    stage([], (*sides[0], (0, -1, 1)))
    sides.append(across([up, down]))
    far = (shifted(up[:half], dz=1), shifted(down[half:], dz=-1))
    slots = row_slots(*after((section_codes, code_owner), scored[-1][3])).astype(jnp.float32)[None]
    far = after(far, *sides[1])
    last = (shifted(far[0], dy=1), shifted(far[1], dy=-1), (Z // 2,))
    stage([([up], -3), ([down], 3)], (*sides[1], (-2, 2)))
    stage([(list(far), Z // 2)], (*sides[2], (-3, 3)))
    stage([], last)

    position = jnp.stack([z, blk * SLOTS]).astype(jnp.int32)
    near = arrange(tuple(groups), position, slots, [s[3] for s in scored])
    stats = [near[:, 0], near[:, 1]]
    passed = shifted(stats[1], dy=-1), shifted(stats[0], dy=1)
    stats = jnp.stack([combine(stats[0], passed[0]), combine(stats[1], passed[1])], axis=1)
    same = [[(y * Z + at) * C + c for at in range(Z)] for y in range(2) for c in range(C)]
    stats = lax.all_to_all(
        jnp.broadcast_to(stats[None], (Z, *stats.shape)), "blk", 0, 0, axis_index_groups=same, tiled=True
    )

    rows = [s[2] for s in scored]
    flipped = position + jnp.stack([0, (1 - 2 * core) * SLOTS]).astype(jnp.int32)
    given = sum_rows(tuple(groups), flipped, near, stats, [s[1] for s in scored], rows)
    taken = [shifted(v, dc=1) for v in given]
    kept = sum_rows(tuple(groups), position, near, stats, [s[0] for s in scored], rows)
    part, slot_part = k // PEERS, SLOTS // PEERS
    got = lax.all_to_all(
        packed_sums(kept, taken).astype(jnp.float16), "dp", split_axis=0, concat_axis=0, tiled=True
    )
    both, cuts = part + slot_part, width // LANES
    full = cuts * both

    def unpacked(values):
        scales = jnp.exp2(values[:, full, :both].astype(jnp.float32))[:, None, :, None]
        return values[:, :full].reshape(PEERS, cuts, both, LANES), scales

    values, scales = unpacked(got)
    sums = jnp.sum(values.astype(jnp.float32) * scales, axis=0)
    counts = got[:, full + 1 : full + 3, :both].astype(jnp.float32)
    counts = jnp.sum(counts, axis=(0, 1))[None, :, None]
    prior = PRIOR * lax.dynamic_slice_in_dim(codebook, peer * part, part).astype(jnp.float32)
    prior = prior.reshape(part, cuts, LANES).transpose(1, 0, 2)
    result = jnp.concatenate(
        [
            (sums[:, :part] + prior) / (counts[:, :part] + PRIOR),
            sums[:, part:] / (counts[:, part:] + 1.0),
        ],
        axis=1,
    )
    size = jnp.max(jnp.abs(result), axis=(0, 2))
    exponent = jnp.clip(jnp.ceil(jnp.log2(jnp.maximum(size, 1e-30))), -100.0, 100.0)
    scaled = (result * jnp.exp2(-exponent)[None, :, None]).reshape(full, LANES)
    sent = jnp.concatenate([scaled.astype(jnp.float16), as_row(exponent)])
    got = lax.all_to_all(
        jnp.broadcast_to(sent[None], (PEERS, *sent.shape)), "dp", split_axis=0, concat_axis=0, tiled=True
    )
    values, scales = unpacked(got)

    def joined(lo, hi):
        rows = jnp.concatenate([values[:, i, lo:hi] for i in range(cuts)], axis=-1)
        return (rows.astype(jnp.float32) * scales[:, 0, lo:hi]).reshape(-1, width)

    return joined(0, part), joined(part, both)


def solution(mesh):
    in_specs = (P(("blk", "dp"), None), P("blk", None), P(("blk", "dp")), P())
    out_specs = (P("blk", None), P("blk", None))
    return jax.shard_map(local, mesh=mesh, in_specs=in_specs, out_specs=out_specs, check_vma=False)
```

```python
import functools
import math

import jax
import jax.numpy as jnp
from jax import lax
from jax.experimental import pallas as pl
from jax.experimental.pallas import tpu as pltpu
from jax.sharding import PartitionSpec as P

SLOTS = 64
X, Y, Z, C = 4, 4, 8, 2
PEERS = X * Y // 2
AXES = ("blk", "dp")
PRIOR = 0.5
MIB = 1 << 20
LANES = 128
TILE = 256


def place(x, y, z, c):
    return ((y % 2 * Z + z) * C + c) * PEERS + x * 2 + y // 2


def chips():
    for x in range(X):
        for y in range(Y):
            for z in range(Z):
                for c in range(C):
                    yield x, y, z, c


def shifted(value, dy=0, dz=0, dc=0):
    pairs = [
        (place(x, y, z, c), place(x, (y + dy) % Y, (z + dz) % Z, (c + dc) % C)) for x, y, z, c in chips()
    ]
    return lax.ppermute(value, AXES, pairs)


def lower_half():
    return lax.broadcasted_iota(jnp.int32, (Z, LANES), 1) < LANES // 2


def score_kernel(plan, count, *refs):
    books, norms, sources = refs[:2], refs[2:4], refs[4 : 4 + count]
    expos, rows, stats = refs[4 + count : 6 + count], refs[6 + count], refs[7 + count]
    k, width = books[0].shape
    n = rows.shape[0]
    for s, a, m, b in plan:
        rows[b : b + m, :] = sources[s][a : a + m, :]
    factor = 2.0 / math.sqrt(width)
    for at in range(0, n, TILE):
        m = min(TILE, n - at)
        block = rows[at : at + m, :]
        scores = [
            (
                lax.dot_general(
                    book[...], block, (((1,), (1,)), ((), ())), preferred_element_type=jnp.float32
                )
                - norm[...]
            )
            * factor
            for book, norm in zip(books, norms)
        ]
        top = jnp.maximum(*(jnp.max(part, axis=0, keepdims=True) for part in scores))
        total = jnp.zeros((1, m), jnp.float32)
        for part, expo in zip(scores, expos):
            value = jnp.exp(part - top)
            total += jnp.sum(value, axis=0, keepdims=True)
            expo[:, at : at + m] = value.astype(jnp.bfloat16)
        for j in range(0, m, LANES):
            g = (at + j) // LANES
            stats[0, g : g + 1, :] = top[:, j : j + LANES]
            stats[1, g : g + 1, :] = total[:, j : j + LANES]


def score_rows(books, norms, sources, plan):
    k, width = books[0].shape
    n = sum(p[2] for p in plan)
    whole = pl.BlockSpec(memory_space=pltpu.VMEM)
    return pl.pallas_call(
        functools.partial(score_kernel, plan, len(sources)),
        in_specs=[whole] * (4 + len(sources)),
        out_specs=(whole,) * 4,
        out_shape=(
            jax.ShapeDtypeStruct((k, n), jnp.bfloat16),
            jax.ShapeDtypeStruct((k, n), jnp.bfloat16),
            jax.ShapeDtypeStruct((n, width), jnp.bfloat16),
            jax.ShapeDtypeStruct((2, n // LANES, LANES), jnp.float32),
        ),
        compiler_params=pltpu.CompilerParams(vmem_limit_bytes=20 * MIB),
        cost_estimate=pl.CostEstimate(
            flops=4 * k * width * n, bytes_accessed=4 * k * width + 4 * k * n, transcendentals=2 * k * n
        ),
    )(*books, *norms, *sources)


def arrange_kernel(groups, position, slots, *refs):
    stats, (out, near, far) = refs[:-3], refs[-3:]
    z = position[0]
    out[2] = jnp.zeros((2, Z, LANES), jnp.float32)
    for which in range(2):
        g = 0
        for stage in stats:
            for i in range(stage.shape[1]):
                side, off = groups[g]
                at = lax.rem(z + off, Z)
                (near, far)[side][pl.ds(at, 1), :] = stage[which, i : i + 1, :]
                g += 1
        out[which, 0] = jnp.where(lower_half(), near[...], far[...])
        out[which, 1] = jnp.where(lower_half(), far[...], near[...])
    first = lax.broadcasted_iota(jnp.int32, (1, LANES), 1) < LANES // 2
    out[2, 0, pl.ds(z, 1), :] = jnp.where(first, slots[...], 0.0)
    out[2, 1, pl.ds(z, 1), :] = jnp.where(first, 0.0, slots[...])


def arrange(groups, position, slots, stats):
    return pl.pallas_call(
        functools.partial(arrange_kernel, groups),
        in_specs=[pl.BlockSpec(memory_space=pltpu.SMEM)]
        + [pl.BlockSpec(memory_space=pltpu.VMEM)] * (1 + len(stats)),
        out_specs=pl.BlockSpec(memory_space=pltpu.VMEM),
        out_shape=jax.ShapeDtypeStruct((3, 2, Z, LANES), jnp.float32),
        scratch_shapes=[pltpu.VMEM((Z, LANES), jnp.float32)] * 2,
        compiler_params=pltpu.CompilerParams(vmem_limit_bytes=4 * MIB),
    )(position, slots, *stats)


def sum_kernel(groups, sizes, position, near, parts, *refs):
    stages = len(sizes)
    expo_in, rows_in = refs[:stages], refs[stages : 2 * stages]
    sums, counts = refs[2 * stages : 2 * stages + 2]
    weights, rows, scale, slot = refs[2 * stages + 2 :]
    k, width = expo_in[0].shape[0], rows.shape[1]
    n = rows.shape[0]
    part, each = k // PEERS, SLOTS // PEERS
    z, first_slot = position[0], position[1]

    def unfolded(pair):
        return jnp.where(lower_half(), pair[0], pair[1]), jnp.where(lower_half(), pair[1], pair[0])

    ratio, number = [], []
    for i in range(2):
        top = functools.reduce(jnp.maximum, [parts[j, 0, i] for j in range(Z)])
        whole = sum(parts[j, 1, i] * jnp.exp(parts[j, 0, i] - top) for j in range(Z))
        ratio.append(jnp.exp(near[0, i] - top) / whole)
        number.append(sum(parts[j, 2, i] for j in range(Z)))
    scale[0], scale[1] = unfolded(ratio)
    slot[0], slot[1] = unfolded(number)

    def line(ref, g):
        side, off = groups[g]
        return ref[side, pl.ds(lax.rem(z + off, Z), 1), :]

    heavy = jnp.zeros((k, LANES), jnp.float32)
    hits = jnp.zeros((LANES, LANES), jnp.float32)
    want = lax.broadcasted_iota(jnp.int32, (LANES, LANES), 0) + first_slot
    total = None
    at, g, done = 0, 0, 0
    for s in range(stages):
        rows[at : at + sizes[s], :] = rows_in[s][...]
        for j in range(0, sizes[s], LANES):
            w = (expo_in[s][:, j : j + LANES].astype(jnp.float32) * line(scale, g)).astype(jnp.bfloat16)
            heavy += w.astype(jnp.float32)
            weights[:k, at + j : at + j + LANES] = w
            hot = jnp.where(want == line(slot, g).astype(jnp.int32), 1.0, 0.0)
            hits += hot
            weights[k:, at + j : at + j + LANES] = hot[:SLOTS].astype(jnp.bfloat16)
            g += 1
        at += sizes[s]
        upto = n if s == stages - 1 else at // TILE * TILE
        if upto - done >= 4 * TILE or upto == n:
            add = jnp.dot(weights[:, done:upto], rows[done:upto, :], preferred_element_type=jnp.float32)
            total = add if total is None else total + add
            done = upto
    for p in range(PEERS):
        sums[p, :part, :] = total[p * part : (p + 1) * part, :]
        sums[p, part:, :] = total[k + p * each : k + (p + 1) * each, :]
    mass = jnp.sum(heavy.T, axis=0, keepdims=True)
    hits = jnp.sum(hits.T, axis=0, keepdims=True)
    blank = jnp.zeros((1, LANES - part - each), jnp.float32)
    for p in range(PEERS):
        counts[p : p + 1, :] = jnp.concatenate(
            [mass[:, p * part : (p + 1) * part], hits[:, p * each : (p + 1) * each], blank], axis=1
        )


def sum_rows(groups, position, near, parts, expos, rows):
    k = expos[0].shape[0]
    width = rows[0].shape[1]
    sizes = tuple(r.shape[0] for r in rows)
    n = sum(sizes)
    in_vmem = pl.BlockSpec(memory_space=pltpu.VMEM)
    return pl.pallas_call(
        functools.partial(sum_kernel, groups, sizes),
        in_specs=[pl.BlockSpec(memory_space=pltpu.SMEM)] + [in_vmem] * (2 + 2 * len(sizes)),
        out_specs=(in_vmem, in_vmem),
        out_shape=(
            jax.ShapeDtypeStruct((PEERS, (k + SLOTS) // PEERS, width), jnp.float32),
            jax.ShapeDtypeStruct((PEERS, LANES), jnp.float32),
        ),
        scratch_shapes=[
            pltpu.VMEM((k + SLOTS, n), jnp.bfloat16),
            pltpu.VMEM((n, width), jnp.bfloat16),
            pltpu.VMEM((2, Z, LANES), jnp.float32),
            pltpu.VMEM((2, Z, LANES), jnp.float32),
        ],
        compiler_params=pltpu.CompilerParams(vmem_limit_bytes=20 * MIB),
        cost_estimate=pl.CostEstimate(
            flops=2 * (k + SLOTS) * width * n, bytes_accessed=2 * k * n + 2 * width * n, transcendentals=0
        ),
    )(position, near, parts, *expos, *rows)


def pack_kernel(kept, taken, kept_counts, taken_counts, out):
    count, width = kept.shape[1:]
    at = count * (width // LANES)
    counts = kept_counts[...] + taken_counts[...]
    high = counts.astype(jnp.bfloat16).astype(jnp.float32)
    low = counts - high
    for p in range(PEERS):
        rows = kept[p] + taken[p]
        size = jnp.max(jnp.abs(rows), axis=1, keepdims=True)
        exponent = jnp.clip(jnp.ceil(jnp.log2(jnp.maximum(size, 1e-30))), -100.0, 100.0)
        rows = rows * jnp.exp2(-exponent)
        for b in range(width // LANES):
            out[p, b * count : (b + 1) * count, :] = rows[:, b * LANES : (b + 1) * LANES]
        wide = jnp.concatenate(
            [jnp.broadcast_to(exponent, (count, LANES)), jnp.zeros((LANES - count, LANES), jnp.float32)]
        )
        out[p, at : at + 1, :] = wide.T[:1, :]
        out[p, at + 1 : at + 2, :] = high[p : p + 1, :]
        out[p, at + 2 : at + 3, :] = low[p : p + 1, :]


def packed_sums(kept, taken):
    _, count, width = kept[0].shape
    in_vmem = pl.BlockSpec(memory_space=pltpu.VMEM)
    return pl.pallas_call(
        pack_kernel,
        in_specs=[in_vmem] * 4,
        out_specs=in_vmem,
        out_shape=jax.ShapeDtypeStruct((PEERS, count * (width // LANES) + 3, LANES), jnp.float32),
        compiler_params=pltpu.CompilerParams(vmem_limit_bytes=8 * MIB),
    )(kept[0], taken[0], kept[1], taken[1])


def combine(first, second):
    top = jnp.maximum(first[0], second[0])
    total = first[1] * jnp.exp(first[0] - top) + second[1] * jnp.exp(second[0] - top)
    return jnp.stack([top, total, first[2] + second[2]])


def row_slots(section_codes, code_owner):
    codes = code_owner.shape[0]
    index = jnp.arange(codes, dtype=jnp.int32)
    same = (code_owner[:, None] == code_owner[None, :]) & (index[None, :] < index[:, None])
    code_slot = code_owner * SLOTS + jnp.sum(same.astype(jnp.int32), axis=1)
    hit = section_codes[:, None] == index[None, :]
    return jnp.sum(jnp.where(hit, code_slot[None, :], 0), axis=1)


def as_row(values):
    pad = [(0, 0)] * (values.ndim - 1) + [(0, LANES - values.shape[-1])]
    return jnp.pad(values, pad)[..., None, :].astype(jnp.float16)


def local(residuals, codebook, section_codes, code_owner):
    blk = lax.axis_index("blk")
    peer = lax.axis_index("dp")
    z, core = blk // C % Z, blk % C
    count, width = residuals.shape
    k = codebook.shape[0]
    half = count // 2

    def norm(book):
        return 0.5 * jnp.sum(jnp.square(book.astype(jnp.float32)), axis=1, keepdims=True)

    up, down = shifted(residuals, dz=1), shifted(residuals, dz=-1)
    other = shifted(codebook, dc=1)
    books, norms = (codebook, other), (norm(codebook), norm(other))

    groups, scored = [], []

    def stage(same, *sides):
        sources, plan, at = [], [], 0
        for block, off in same:
            for piece in block:
                plan.append((len(sources), 0, piece.shape[0], at))
                sources.append(piece)
                at += piece.shape[0]
            groups.append((0, off % Z))
        for lower, upper, offs in sides:
            first = len(sources)
            sources.extend((lower, upper))
            for i, off in enumerate(offs):
                plan += [(first, i * half, half, at), (first + 1, i * half, half, at + half)]
                at += count
                groups.append((1, off % Z))
        scored.append(score_rows(books, norms, sources, tuple(plan)))

    def after(value, *earlier):
        return lax.optimization_barrier((value, earlier))[0]

    def across(blocks, *earlier):
        parts = after(
            (jnp.concatenate([b[:half] for b in blocks]), jnp.concatenate([b[half:] for b in blocks])), *earlier
        )
        return shifted(parts[0], dy=1), shifted(parts[1], dy=-1)

    stage([([up], -1), ([down], 1)])
    near_side = across([residuals, up, down], scored[-1][3])
    up_two, down_two = after((shifted(up, dz=1), shifted(down, dz=-1)), scored[-1][3])
    stage([([up_two], -2), ([down_two], 2)])
    up, down = after((shifted(up_two, dz=1), shifted(down_two, dz=-1)), scored[-1][3])
    far = (shifted(up[:half], dz=1), shifted(down[half:], dz=-1))
    side = across([up_two, down_two, up, down])
    stage([([residuals], 0)], (*near_side, (0, -1, 1)))
    slots = row_slots(*after((section_codes, code_owner), scored[-1][3])).astype(jnp.float32)[None]
    far = after(far, scored[-1][3])
    far_side = (shifted(far[0], dy=1), shifted(far[1], dy=-1))
    up, down = after((up, down), scored[-1][3])
    stage([([up], -3), ([down], 3)])
    stage([], (*side, (-2, 2, -3, 3)))
    far_side = after(far_side, scored[-1][3])
    stage([(list(far), Z // 2)], (*far_side, (Z // 2,)))

    position = jnp.stack([z, blk * SLOTS]).astype(jnp.int32)
    near = arrange(tuple(groups), position, slots, [s[3] for s in scored])
    stats = [near[:, 0], near[:, 1]]
    passed = shifted(stats[1], dy=-1), shifted(stats[0], dy=1)
    stats = jnp.stack([combine(stats[0], passed[0]), combine(stats[1], passed[1])], axis=1)
    same = [[(y * Z + at) * C + c for at in range(Z)] for y in range(2) for c in range(C)]
    stats = lax.all_to_all(
        jnp.broadcast_to(stats[None], (Z, *stats.shape)), "blk", 0, 0, axis_index_groups=same, tiled=True
    )

    rows = [s[2] for s in scored]
    flipped = position + jnp.stack([0, (1 - 2 * core) * SLOTS]).astype(jnp.int32)
    given = sum_rows(tuple(groups), flipped, near, stats, [s[1] for s in scored], rows)
    taken = [shifted(v, dc=1) for v in given]
    kept = sum_rows(tuple(groups), position, near, stats, [s[0] for s in scored], rows)
    part, slot_part = k // PEERS, SLOTS // PEERS
    got = lax.all_to_all(
        packed_sums(kept, taken).astype(jnp.float16), "dp", split_axis=0, concat_axis=0, tiled=True
    )
    both, cuts = part + slot_part, width // LANES
    full = cuts * both

    def unpacked(values):
        scales = jnp.exp2(values[:, full, :both].astype(jnp.float32))[:, None, :, None]
        return values[:, :full].reshape(PEERS, cuts, both, LANES), scales

    values, scales = unpacked(got)
    sums = jnp.sum(values.astype(jnp.float32) * scales, axis=0)
    counts = got[:, full + 1 : full + 3, :both].astype(jnp.float32)
    counts = jnp.sum(counts, axis=(0, 1))[None, :, None]
    prior = PRIOR * lax.dynamic_slice_in_dim(codebook, peer * part, part).astype(jnp.float32)
    prior = prior.reshape(part, cuts, LANES).transpose(1, 0, 2)
    result = jnp.concatenate(
        [
            (sums[:, :part] + prior) / (counts[:, :part] + PRIOR),
            sums[:, part:] / (counts[:, part:] + 1.0),
        ],
        axis=1,
    )
    size = jnp.max(jnp.abs(result), axis=(0, 2))
    exponent = jnp.clip(jnp.ceil(jnp.log2(jnp.maximum(size, 1e-30))), -100.0, 100.0)
    scaled = (result * jnp.exp2(-exponent)[None, :, None]).reshape(full, LANES)
    sent = jnp.concatenate([scaled.astype(jnp.float16), as_row(exponent)])
    got = lax.all_to_all(
        jnp.broadcast_to(sent[None], (PEERS, *sent.shape)), "dp", split_axis=0, concat_axis=0, tiled=True
    )
    values, scales = unpacked(got)

    def joined(lo, hi):
        rows = jnp.concatenate([values[:, i, lo:hi] for i in range(cuts)], axis=-1)
        return (rows.astype(jnp.float32) * scales[:, 0, lo:hi]).reshape(-1, width)

    return joined(0, part), joined(part, both)


def solution(mesh):
    in_specs = (P(("blk", "dp"), None), P("blk", None), P(("blk", "dp")), P())
    out_specs = (P("blk", None), P("blk", None))
    return jax.shard_map(local, mesh=mesh, in_specs=in_specs, out_specs=out_specs, check_vma=False)
```

```python
import functools
import math

import jax
import jax.numpy as jnp
from jax import lax
from jax.experimental import pallas as pl
from jax.experimental.pallas import tpu as pltpu
from jax.sharding import PartitionSpec as P

SLOTS = 64
X, Y, Z, C = 4, 4, 8, 2
PEERS = X * Y // 2
AXES = ("blk", "dp")
PRIOR = 0.5
MIB = 1 << 20
LANES = 128
TILE = 256


def place(x, y, z, c):
    return ((y % 2 * Z + z) * C + c) * PEERS + x * 2 + y // 2


def chips():
    for x in range(X):
        for y in range(Y):
            for z in range(Z):
                for c in range(C):
                    yield x, y, z, c


def shifted(value, dy=0, dz=0, dc=0):
    pairs = [
        (place(x, y, z, c), place(x, (y + dy) % Y, (z + dz) % Z, (c + dc) % C)) for x, y, z, c in chips()
    ]
    return lax.ppermute(value, AXES, pairs)


def lower_half():
    return lax.broadcasted_iota(jnp.int32, (Z, LANES), 1) < LANES // 2


def score_kernel(plan, count, *refs):
    books, norms, sources = refs[:2], refs[2:4], refs[4 : 4 + count]
    expos, rows, stats = refs[4 + count : 6 + count], refs[6 + count], refs[7 + count]
    k, width = books[0].shape
    n = rows.shape[0]
    for s, a, m, b in plan:
        rows[b : b + m, :] = sources[s][a : a + m, :]
    factor = 2.0 / math.sqrt(width) * math.log2(math.e)
    for at in range(0, n, TILE):
        m = min(TILE, n - at)
        block = rows[at : at + m, :]
        scores = [
            (
                lax.dot_general(
                    book[...], block, (((1,), (1,)), ((), ())), preferred_element_type=jnp.float32
                )
                - norm[...]
            )
            * factor
            for book, norm in zip(books, norms)
        ]
        top = jnp.maximum(*(jnp.max(part, axis=0, keepdims=True) for part in scores))
        total = jnp.zeros((1, m), jnp.float32)
        for part, expo in zip(scores, expos):
            value = jnp.exp2(part - top)
            total += jnp.sum(value, axis=0, keepdims=True)
            expo[:, at : at + m] = value.astype(jnp.bfloat16)
        for j in range(0, m, LANES):
            g = (at + j) // LANES
            stats[0, g : g + 1, :] = top[:, j : j + LANES]
            stats[1, g : g + 1, :] = total[:, j : j + LANES]


def score_rows(books, norms, sources, plan):
    k, width = books[0].shape
    n = sum(p[2] for p in plan)
    whole = pl.BlockSpec(memory_space=pltpu.VMEM)
    return pl.pallas_call(
        functools.partial(score_kernel, plan, len(sources)),
        in_specs=[whole] * (4 + len(sources)),
        out_specs=(whole,) * 4,
        out_shape=(
            jax.ShapeDtypeStruct((k, n), jnp.bfloat16),
            jax.ShapeDtypeStruct((k, n), jnp.bfloat16),
            jax.ShapeDtypeStruct((n, width), jnp.bfloat16),
            jax.ShapeDtypeStruct((2, n // LANES, LANES), jnp.float32),
        ),
        compiler_params=pltpu.CompilerParams(vmem_limit_bytes=20 * MIB),
        cost_estimate=pl.CostEstimate(
            flops=4 * k * width * n, bytes_accessed=4 * k * width + 4 * k * n, transcendentals=2 * k * n
        ),
    )(*books, *norms, *sources)


def arrange_kernel(groups, position, slots, *refs):
    stats, (out, near, far) = refs[:-3], refs[-3:]
    z = position[0]
    out[2] = jnp.zeros((2, Z, LANES), jnp.float32)
    for which in range(2):
        g = 0
        for stage in stats:
            for i in range(stage.shape[1]):
                side, off = groups[g]
                at = lax.rem(z + off, Z)
                (near, far)[side][pl.ds(at, 1), :] = stage[which, i : i + 1, :]
                g += 1
        out[which, 0] = jnp.where(lower_half(), near[...], far[...])
        out[which, 1] = jnp.where(lower_half(), far[...], near[...])
    first = lax.broadcasted_iota(jnp.int32, (1, LANES), 1) < LANES // 2
    out[2, 0, pl.ds(z, 1), :] = jnp.where(first, slots[...], 0.0)
    out[2, 1, pl.ds(z, 1), :] = jnp.where(first, 0.0, slots[...])


def arrange(groups, position, slots, stats):
    return pl.pallas_call(
        functools.partial(arrange_kernel, groups),
        in_specs=[pl.BlockSpec(memory_space=pltpu.SMEM)]
        + [pl.BlockSpec(memory_space=pltpu.VMEM)] * (1 + len(stats)),
        out_specs=pl.BlockSpec(memory_space=pltpu.VMEM),
        out_shape=jax.ShapeDtypeStruct((3, 2, Z, LANES), jnp.float32),
        scratch_shapes=[pltpu.VMEM((Z, LANES), jnp.float32)] * 2,
        compiler_params=pltpu.CompilerParams(vmem_limit_bytes=4 * MIB),
    )(position, slots, *stats)


def sum_kernel(groups, sizes, position, near, parts, *refs):
    stages = len(sizes)
    expo_in, rows_in = refs[:stages], refs[stages : 2 * stages]
    sums, counts = refs[2 * stages : 2 * stages + 2]
    weights, rows, scale, slot = refs[2 * stages + 2 :]
    k, width = expo_in[0].shape[0], rows.shape[1]
    n = rows.shape[0]
    part, each = k // PEERS, SLOTS // PEERS
    z, first_slot = position[0], position[1]

    def unfolded(pair):
        return jnp.where(lower_half(), pair[0], pair[1]), jnp.where(lower_half(), pair[1], pair[0])

    ratio, number = [], []
    for i in range(2):
        top = functools.reduce(jnp.maximum, [parts[j, 0, i] for j in range(Z)])
        whole = sum(parts[j, 1, i] * jnp.exp2(parts[j, 0, i] - top) for j in range(Z))
        ratio.append(jnp.exp2(near[0, i] - top) / whole)
        number.append(sum(parts[j, 2, i] for j in range(Z)))
    scale[0], scale[1] = unfolded(ratio)
    slot[0], slot[1] = unfolded(number)

    def line(ref, g):
        side, off = groups[g]
        return ref[side, pl.ds(lax.rem(z + off, Z), 1), :]

    heavy = jnp.zeros((k, LANES), jnp.float32)
    hits = jnp.zeros((LANES, LANES), jnp.float32)
    want = lax.broadcasted_iota(jnp.int32, (LANES, LANES), 0) + first_slot
    total = None
    at, g, done = 0, 0, 0
    for s in range(stages):
        rows[at : at + sizes[s], :] = rows_in[s][...]
        for j in range(0, sizes[s], LANES):
            w = (expo_in[s][:, j : j + LANES].astype(jnp.float32) * line(scale, g)).astype(jnp.bfloat16)
            heavy += w.astype(jnp.float32)
            weights[:k, at + j : at + j + LANES] = w
            hot = jnp.where(want == line(slot, g).astype(jnp.int32), 1.0, 0.0)
            hits += hot
            weights[k:, at + j : at + j + LANES] = hot[:SLOTS].astype(jnp.bfloat16)
            g += 1
        at += sizes[s]
        upto = n if s == stages - 1 else at // TILE * TILE
        if upto - done >= 4 * TILE or upto == n:
            add = jnp.dot(weights[:, done:upto], rows[done:upto, :], preferred_element_type=jnp.float32)
            total = add if total is None else total + add
            done = upto
    for p in range(PEERS):
        sums[p, :part, :] = total[p * part : (p + 1) * part, :]
        sums[p, part:, :] = total[k + p * each : k + (p + 1) * each, :]
    mass = jnp.sum(heavy.T, axis=0, keepdims=True)
    hits = jnp.sum(hits.T, axis=0, keepdims=True)
    blank = jnp.zeros((1, LANES - part - each), jnp.float32)
    for p in range(PEERS):
        counts[p : p + 1, :] = jnp.concatenate(
            [mass[:, p * part : (p + 1) * part], hits[:, p * each : (p + 1) * each], blank], axis=1
        )


def sum_rows(groups, position, near, parts, expos, rows):
    k = expos[0].shape[0]
    width = rows[0].shape[1]
    sizes = tuple(r.shape[0] for r in rows)
    n = sum(sizes)
    in_vmem = pl.BlockSpec(memory_space=pltpu.VMEM)
    return pl.pallas_call(
        functools.partial(sum_kernel, groups, sizes),
        in_specs=[pl.BlockSpec(memory_space=pltpu.SMEM)] + [in_vmem] * (2 + 2 * len(sizes)),
        out_specs=(in_vmem, in_vmem),
        out_shape=(
            jax.ShapeDtypeStruct((PEERS, (k + SLOTS) // PEERS, width), jnp.float32),
            jax.ShapeDtypeStruct((PEERS, LANES), jnp.float32),
        ),
        scratch_shapes=[
            pltpu.VMEM((k + SLOTS, n), jnp.bfloat16),
            pltpu.VMEM((n, width), jnp.bfloat16),
            pltpu.VMEM((2, Z, LANES), jnp.float32),
            pltpu.VMEM((2, Z, LANES), jnp.float32),
        ],
        compiler_params=pltpu.CompilerParams(vmem_limit_bytes=20 * MIB),
        cost_estimate=pl.CostEstimate(
            flops=2 * (k + SLOTS) * width * n, bytes_accessed=2 * k * n + 2 * width * n, transcendentals=0
        ),
    )(position, near, parts, *expos, *rows)


def pack_kernel(kept, taken, kept_counts, taken_counts, out):
    count, width = kept.shape[1:]
    at = count * (width // LANES)
    counts = kept_counts[...] + taken_counts[...]
    high = counts.astype(jnp.bfloat16).astype(jnp.float32)
    low = counts - high
    for p in range(PEERS):
        rows = kept[p] + taken[p]
        size = jnp.max(jnp.abs(rows), axis=1, keepdims=True)
        exponent = jnp.clip(jnp.ceil(jnp.log2(jnp.maximum(size, 1e-30))), -100.0, 100.0)
        rows = rows * jnp.exp2(-exponent)
        for b in range(width // LANES):
            out[p, b * count : (b + 1) * count, :] = rows[:, b * LANES : (b + 1) * LANES]
        wide = jnp.concatenate(
            [jnp.broadcast_to(exponent, (count, LANES)), jnp.zeros((LANES - count, LANES), jnp.float32)]
        )
        out[p, at : at + 1, :] = wide.T[:1, :]
        out[p, at + 1 : at + 2, :] = high[p : p + 1, :]
        out[p, at + 2 : at + 3, :] = low[p : p + 1, :]


def packed_sums(kept, taken):
    _, count, width = kept[0].shape
    in_vmem = pl.BlockSpec(memory_space=pltpu.VMEM)
    return pl.pallas_call(
        pack_kernel,
        in_specs=[in_vmem] * 4,
        out_specs=in_vmem,
        out_shape=jax.ShapeDtypeStruct((PEERS, count * (width // LANES) + 3, LANES), jnp.float32),
        compiler_params=pltpu.CompilerParams(vmem_limit_bytes=8 * MIB),
    )(kept[0], taken[0], kept[1], taken[1])


def combine(first, second):
    top = jnp.maximum(first[0], second[0])
    total = first[1] * jnp.exp2(first[0] - top) + second[1] * jnp.exp2(second[0] - top)
    return jnp.stack([top, total, first[2] + second[2]])


def row_slots(section_codes, code_owner):
    codes = code_owner.shape[0]
    index = jnp.arange(codes, dtype=jnp.int32)
    same = (code_owner[:, None] == code_owner[None, :]) & (index[None, :] < index[:, None])
    code_slot = code_owner * SLOTS + jnp.sum(same.astype(jnp.int32), axis=1)
    hit = section_codes[:, None] == index[None, :]
    return jnp.sum(jnp.where(hit, code_slot[None, :], 0), axis=1)


def as_row(values):
    pad = [(0, 0)] * (values.ndim - 1) + [(0, LANES - values.shape[-1])]
    return jnp.pad(values, pad)[..., None, :].astype(jnp.float16)


def local(residuals, codebook, section_codes, code_owner):
    blk = lax.axis_index("blk")
    peer = lax.axis_index("dp")
    z, core = blk // C % Z, blk % C
    count, width = residuals.shape
    k = codebook.shape[0]
    half = count // 2

    def norm(book):
        return 0.5 * jnp.sum(jnp.square(book.astype(jnp.float32)), axis=1, keepdims=True)

    up, down = shifted(residuals, dz=1), shifted(residuals, dz=-1)
    other = shifted(codebook, dc=1)
    books, norms = (codebook, other), (norm(codebook), norm(other))

    groups, scored = [], []

    def stage(same, *sides):
        sources, plan, at = [], [], 0
        for block, off in same:
            for piece in block:
                plan.append((len(sources), 0, piece.shape[0], at))
                sources.append(piece)
                at += piece.shape[0]
            groups.append((0, off % Z))
        for lower, upper, offs in sides:
            first = len(sources)
            sources.extend((lower, upper))
            for i, off in enumerate(offs):
                plan += [(first, i * half, half, at), (first + 1, i * half, half, at + half)]
                at += count
                groups.append((1, off % Z))
        scored.append(score_rows(books, norms, sources, tuple(plan)))

    def after(value, *earlier):
        return lax.optimization_barrier((value, earlier))[0]

    def across(blocks, *earlier):
        parts = after(
            (jnp.concatenate([b[:half] for b in blocks]), jnp.concatenate([b[half:] for b in blocks])), *earlier
        )
        return shifted(parts[0], dy=1), shifted(parts[1], dy=-1)

    stage([([up], -1), ([down], 1)])
    near_side = across([residuals, up, down], scored[-1][3])
    up_two, down_two = after((shifted(up, dz=1), shifted(down, dz=-1)), scored[-1][3])
    stage([([up_two], -2), ([down_two], 2)])
    up, down = after((shifted(up_two, dz=1), shifted(down_two, dz=-1)), scored[-1][3])
    far = (shifted(up[:half], dz=1), shifted(down[half:], dz=-1))
    side = across([up_two, down_two, up, down])
    stage([([residuals], 0)], (*near_side, (0, -1, 1)))
    slots = row_slots(*after((section_codes, code_owner), scored[-1][3])).astype(jnp.float32)[None]
    far = after(far, scored[-1][3])
    far_side = (shifted(far[0], dy=1), shifted(far[1], dy=-1))
    up, down = after((up, down), scored[-1][3])
    stage([([up], -3), ([down], 3)])
    stage([], (*side, (-2, 2, -3, 3)))
    far_side = after(far_side, scored[-1][3])
    stage([(list(far), Z // 2)], (*far_side, (Z // 2,)))

    position = jnp.stack([z, blk * SLOTS]).astype(jnp.int32)
    near = arrange(tuple(groups), position, slots, [s[3] for s in scored])
    stats = [near[:, 0], near[:, 1]]
    passed = shifted(stats[1], dy=-1), shifted(stats[0], dy=1)
    stats = jnp.stack([combine(stats[0], passed[0]), combine(stats[1], passed[1])], axis=1)
    same = [[(y * Z + at) * C + c for at in range(Z)] for y in range(2) for c in range(C)]
    stats = lax.all_to_all(
        jnp.broadcast_to(stats[None], (Z, *stats.shape)), "blk", 0, 0, axis_index_groups=same, tiled=True
    )

    rows = [s[2] for s in scored]
    flipped = position + jnp.stack([0, (1 - 2 * core) * SLOTS]).astype(jnp.int32)
    given = sum_rows(tuple(groups), flipped, near, stats, [s[1] for s in scored], rows)
    taken = [shifted(v, dc=1) for v in given]
    kept = sum_rows(tuple(groups), position, near, stats, [s[0] for s in scored], rows)
    part, slot_part = k // PEERS, SLOTS // PEERS
    got = lax.all_to_all(
        packed_sums(kept, taken).astype(jnp.float16), "dp", split_axis=0, concat_axis=0, tiled=True
    )
    both, cuts = part + slot_part, width // LANES
    full = cuts * both

    def unpacked(values):
        scales = jnp.exp2(values[:, full, :both].astype(jnp.float32))[:, None, :, None]
        return values[:, :full].reshape(PEERS, cuts, both, LANES), scales

    values, scales = unpacked(got)
    sums = jnp.sum(values.astype(jnp.float32) * scales, axis=0)
    counts = got[:, full + 1 : full + 3, :both].astype(jnp.float32)
    counts = jnp.sum(counts, axis=(0, 1))[None, :, None]
    prior = PRIOR * lax.dynamic_slice_in_dim(codebook, peer * part, part).astype(jnp.float32)
    prior = prior.reshape(part, cuts, LANES).transpose(1, 0, 2)
    result = jnp.concatenate(
        [
            (sums[:, :part] + prior) / (counts[:, :part] + PRIOR),
            sums[:, part:] / (counts[:, part:] + 1.0),
        ],
        axis=1,
    )
    size = jnp.max(jnp.abs(result), axis=(0, 2))
    exponent = jnp.clip(jnp.ceil(jnp.log2(jnp.maximum(size, 1e-30))), -100.0, 100.0)
    scaled = (result * jnp.exp2(-exponent)[None, :, None]).reshape(full, LANES)
    sent = jnp.concatenate([scaled.astype(jnp.float16), as_row(exponent)])
    got = lax.all_to_all(
        jnp.broadcast_to(sent[None], (PEERS, *sent.shape)), "dp", split_axis=0, concat_axis=0, tiled=True
    )
    values, scales = unpacked(got)

    def joined(lo, hi):
        rows = jnp.concatenate([values[:, i, lo:hi] for i in range(cuts)], axis=-1)
        return (rows.astype(jnp.float32) * scales[:, 0, lo:hi]).reshape(-1, width)

    return joined(0, part), joined(part, both)


def solution(mesh):
    in_specs = (P(("blk", "dp"), None), P("blk", None), P(("blk", "dp")), P())
    out_specs = (P("blk", None), P("blk", None))
    return jax.shard_map(local, mesh=mesh, in_specs=in_specs, out_specs=out_specs, check_vma=False)
```
